128 devices in a mesh: lat: 8 (over x, core), lon: 16 (over y, z).
Axes of the slice: x: 4, y: 4, z: 4, core: 2. Of those that a mesh axis runs over, the one named last changes fastest.
Arguments:
- node_latent: bfloat16 [32768, 512], P(('lat', 'lon')), may hold values from -6 to 6
- edge_latent: bfloat16 [262144, 512], P(('lat', 'lon')), may hold values from -6 to 6
- sender_slot: int32 [262144], P(('lat', 'lon')), may hold values from 0 to 1279, as said below
- receiver: int32 [262144], P(('lat', 'lon')), may hold values from 0 to 255
- border_list: int32 [128, 2, 2, 32], P(('lat', 'lon')), may hold values from 0 to 255
- send_list: int32 [128, 128, 4], P(('lat', 'lon')), may hold values from 0 to 255
- edge_count: int32 [128], P(('lat', 'lon')), may hold values from 1024 to 2048, as said below
- edge_weight: bfloat16 [512, 512], replicated, may hold values from -0.25 to 0.25
- sender_weight: bfloat16 [512, 512], replicated, may hold values from -0.25 to 0.25
- receiver_weight: bfloat16 [512, 512], replicated, may hold values from -0.25 to 0.25
- hidden_bias: float32 [512], replicated, may hold values from -3 to 3
- message_weight: bfloat16 [512, 512], replicated, may hold values from -0.25 to 0.25
- message_bias: float32 [512], replicated, may hold values from -3 to 3
- edge_scales: float32 [512], replicated, may hold values from 0.25 to 1.75
- self_weight: bfloat16 [512, 512], replicated, may hold values from -0.25 to 0.25
- summed_weight: bfloat16 [512, 512], replicated, may hold values from -0.25 to 0.25
- node_bias: float32 [512], replicated, may hold values from -3 to 3
- update_weight: bfloat16 [512, 512], replicated, may hold values from -0.25 to 0.25
- update_bias: float32 [512], replicated, may hold values from -3 to 3
- node_scales: float32 [512], replicated, may hold values from 0.25 to 1.75
- node_cotangent: bfloat16 [32768, 512], P(('lat', 'lon')), may hold values from -6 to 6
- edge_cotangent: bfloat16 [262144, 512], P(('lat', 'lon')), may hold values from -6 to 6
Outputs:
- node_result: bfloat16 [32768, 512], P(('lat', 'lon'))
- edge_result: bfloat16 [262144, 512], P(('lat', 'lon'))
- node_grad: float32 [32768, 512], P(('lat', 'lon'))
- edge_grad: float32 [262144, 512], P(('lat', 'lon'))
The draws below stay inside these ranges and needn't reach their ends.
Inputs may be any that keep to these rules, and one draw needn't show every extreme that they name: `sender_slot`: most edges take a sender from their own partition's rows, most others from the border block; border cells beyond the latitude ends are never named. `border_list`: rows of one border group may repeat. `send_list`: rows of one send list may repeat. `edge_count`: some partition has all 2048 slots live.
All inputs are finite; a program needn't handle non-finite values.
Results may differ from the reference program's by a relative error of at most 0.015.
Values may be sent and summed in bfloat16 or wider, within the bound.
A program may use at most 128 MiB of HBM per device.

```python
import jax
import jax.numpy as jnp
from jax import lax

D = 512
NODE_DEV = 256
HALO = 32
CAP = 4
EDGE_PER_SHARD = 2048
NODES = 32768
EDGES = 262144
N_LAT = 8
N_LON = 16
DEVICES = 128


def draw_edge_count(key, part):
    key = jax.random.fold_in(key, 7)
    first_key, second_key = jax.random.split(key)
    counts = jax.random.randint(first_key, (DEVICES,), EDGE_PER_SHARD // 2, EDGE_PER_SHARD + 1, dtype=jnp.int32)
    fullest = jax.random.randint(second_key, (), 0, DEVICES, dtype=jnp.int32)
    return counts.at[fullest].set(EDGE_PER_SHARD)


def draw_sender_slot(key, part):
    key = jax.random.fold_in(key, 11)
    keys = jax.random.split(key, 7)
    owner = jnp.arange(EDGES, dtype=jnp.int32) // EDGE_PER_SHARD
    band = owner // N_LON
    bands = DEVICES // N_LON
    kind = jax.random.randint(keys[0], (EDGES,), 0, 100, dtype=jnp.int32)
    own_row = jax.random.randint(keys[1], (EDGES,), 0, NODE_DEV, dtype=jnp.int32)
    cells = jnp.array([0, 1, 2, 3, 4, 7, 8, 11, 12, 13, 14, 15], dtype=jnp.int32)
    code = cells[jax.random.randint(keys[2], (EDGES,), 0, 12, dtype=jnp.int32)]
    row_cell = code // 4
    col_cell = code % 4
    row_cell = jnp.where((band == 0) & (row_cell == 0), 1, row_cell)
    row_cell = jnp.where((band == bands - 1) & (row_cell == 3), 2, row_cell)
    border_row = jax.random.randint(keys[3], (EDGES,), 0, HALO, dtype=jnp.int32)
    border_index = NODE_DEV + (row_cell * 4 + col_cell) * HALO + border_row
    far_table = jax.random.randint(keys[4], (DEVICES, 6), 0, DEVICES, dtype=jnp.int32)
    pick = jax.random.randint(keys[5], (EDGES,), 0, 6, dtype=jnp.int32)
    source = far_table[owner, pick]
    far_row = jax.random.randint(keys[6], (EDGES,), 0, CAP, dtype=jnp.int32)
    far_index = NODE_DEV + 16 * HALO + source * CAP + far_row
    result = jnp.where(kind < 74, own_row, jnp.where(kind < 92, border_index, far_index))
    result = result.at[0].set(0)
    return result.at[EDGES - 1].set(NODE_DEV + 16 * HALO + DEVICES * CAP - 1)


def place_ends(drawn, own_key, smallest, largest):
    longest = drawn.shape.index(max(drawn.shape))
    spots = []
    for shift in (0, 1):
        where = [jax.random.randint(jax.random.fold_in(own_key, axis), (), 0, length) for axis, length in enumerate(drawn.shape)]
        where[longest] = (where[longest] + shift) % drawn.shape[longest]
        spots.append(tuple(where))
    return drawn.at[spots[0]].set(smallest).at[spots[1]].set(largest)


def levels(key, extent, shards, least, high):
    def one(axis_at, shards_of):
        draws = jax.random.uniform(jax.random.fold_in(jax.random.fold_in(key, 6), axis_at), (shards_of,), jnp.float32, least / len(shards), high / len(shards))
        return jnp.repeat(jnp.exp(draws), extent[axis_at] // shards_of).reshape((-1,) + (1,) * (len(extent) - axis_at - 1))

    level = one(*shards[0])
    for cut in shards[1:]:
        level = level * one(*cut)
    return level


def bell_draw(key, dims, scale, reach, pieces=(), held_as=jnp.bfloat16):
    drawn = jax.random.normal(key, dims, jnp.float32) * scale
    if len(pieces) > 0:
        drawn = levels(key, dims, pieces, -0.22, 0.18) * drawn
    return jnp.clip(drawn, min=-reach, max=reach).astype(held_as)


def setup_inputs(seed: int = 0) -> dict:
    arg_keys = jax.random.split(jax.random.key(seed), 23)
    node_latent = bell_draw(arg_keys[0], (NODES, D), 1.0, 6.0, ((0, 128),))
    edge_latent = bell_draw(arg_keys[1], (EDGES, D), 1.0, 6.0, ((0, 128),))
    sender_slot = draw_sender_slot(jax.random.fold_in(arg_keys[22], 71), 0)
    receiver = place_ends(jax.random.randint(arg_keys[3], (EDGES,), 0, NODE_DEV), jax.random.fold_in(arg_keys[3], 1), 0, NODE_DEV - 1).astype(jnp.int32)
    border_list = place_ends(jax.random.randint(arg_keys[4], (DEVICES, 2, 2, HALO), 0, NODE_DEV), jax.random.fold_in(arg_keys[4], 1), 0, NODE_DEV - 1).astype(jnp.int32)
    send_list = place_ends(jax.random.randint(arg_keys[5], (DEVICES, DEVICES, CAP), 0, NODE_DEV), jax.random.fold_in(arg_keys[5], 1), 0, NODE_DEV - 1).astype(jnp.int32)
    edge_count = draw_edge_count(jax.random.fold_in(arg_keys[22], 71), 0)
    edge_weight = bell_draw(arg_keys[7], (D, D), D ** -0.5, 0.25)
    sender_weight = bell_draw(arg_keys[8], (D, D), D ** -0.5, 0.25)
    receiver_weight = bell_draw(arg_keys[9], (D, D), D ** -0.5, 0.25)
    hidden_bias = bell_draw(arg_keys[10], (D,), 0.5, 3.0, (), jnp.float32)
    message_weight = bell_draw(arg_keys[11], (D, D), D ** -0.5, 0.25)
    message_bias = bell_draw(arg_keys[12], (D,), 0.5, 3.0, (), jnp.float32)
    edge_scales = jnp.clip(1.0 + 0.15 * jax.random.normal(arg_keys[13], (D,), jnp.float32), 0.25, 1.75)
    self_weight = bell_draw(arg_keys[14], (D, D), D ** -0.5, 0.25)
    summed_weight = bell_draw(arg_keys[15], (D, D), D ** -0.5, 0.25)
    node_bias = bell_draw(arg_keys[16], (D,), 0.5, 3.0, (), jnp.float32)
    update_weight = bell_draw(arg_keys[17], (D, D), D ** -0.5, 0.25)
    update_bias = bell_draw(arg_keys[18], (D,), 0.5, 3.0, (), jnp.float32)
    node_scales = jnp.clip(1.0 + 0.15 * jax.random.normal(arg_keys[19], (D,), jnp.float32), 0.25, 1.75)
    node_cotangent = bell_draw(arg_keys[20], (NODES, D), 1.0, 6.0, ((0, 128),))
    edge_cotangent = bell_draw(arg_keys[21], (EDGES, D), 1.0, 6.0, ((0, 128),))
    return dict(node_latent=node_latent, edge_latent=edge_latent, sender_slot=sender_slot, receiver=receiver, border_list=border_list, send_list=send_list, edge_count=edge_count, edge_weight=edge_weight, sender_weight=sender_weight, receiver_weight=receiver_weight, hidden_bias=hidden_bias, message_weight=message_weight, message_bias=message_bias, edge_scales=edge_scales, self_weight=self_weight, summed_weight=summed_weight, node_bias=node_bias, update_weight=update_weight, update_bias=update_bias, node_scales=node_scales, node_cotangent=node_cotangent, edge_cotangent=edge_cotangent)


def layer_norm(values, scales):
    average = lax.optimization_barrier(jnp.mean(values, -1, keepdims=True))
    centred = values - average
    scatter_result = lax.optimization_barrier(jnp.mean(centred * centred, -1, keepdims=True))
    return centred * lax.rsqrt(scatter_result + 1e-05) * scales

def local_layer(node_wide, table, edge_widened, sender_slot, receiver, active_count, weights):
    edge_weight, sender_weight, receiver_weight, hidden_bias, message_weight, message_bias, edge_scales, self_weight, summed_weight, node_bias, update_weight, update_bias, node_scales = weights
    sender_rows = table[sender_slot]
    receiver_rows = node_wide[receiver]
    hidden = jnp.dot(edge_widened.astype(jnp.bfloat16), edge_weight, preferred_element_type=jnp.float32) + jnp.dot(sender_rows.astype(jnp.bfloat16), sender_weight, preferred_element_type=jnp.float32) + jnp.dot(receiver_rows.astype(jnp.bfloat16), receiver_weight, preferred_element_type=jnp.float32) + hidden_bias
    hidden = jax.nn.silu(hidden).astype(jnp.bfloat16)
    edge_message = layer_norm(jnp.dot(hidden, message_weight, preferred_element_type=jnp.float32) + message_bias, edge_scales)
    active_mask = (jnp.arange(edge_widened.shape[0], dtype=jnp.int32) < active_count).astype(jnp.float32)
    edge_message = edge_message * active_mask[:, None]
    edge_result = (edge_widened + edge_message).astype(jnp.bfloat16)
    one_hot = (receiver[None, :] == jnp.arange(node_wide.shape[0], dtype=jnp.int32)[:, None]).astype(jnp.bfloat16)
    summed = jnp.dot(one_hot, edge_message.astype(jnp.bfloat16), preferred_element_type=jnp.float32).astype(jnp.bfloat16)
    inner = jnp.dot(node_wide.astype(jnp.bfloat16), self_weight, preferred_element_type=jnp.float32) + jnp.dot(summed, summed_weight, preferred_element_type=jnp.float32) + node_bias
    inner = jax.nn.silu(inner).astype(jnp.bfloat16)
    update = layer_norm(jnp.dot(inner, update_weight, preferred_element_type=jnp.float32) + update_bias, node_scales)
    node_result = (node_wide + update).astype(jnp.bfloat16)
    return (node_result, edge_result)

def reference(node_latent, edge_latent, sender_slot, receiver, border_list, send_list, edge_count, edge_weight, sender_weight, receiver_weight, hidden_bias, message_weight, message_bias, edge_scales, self_weight, summed_weight, node_bias, update_weight, update_bias, node_scales, node_cotangent, edge_cotangent):
    weights = (edge_weight, sender_weight, receiver_weight, hidden_bias, message_weight, message_bias, edge_scales, self_weight, summed_weight, node_bias, update_weight, update_bias, node_scales)
    sources = jnp.arange(DEVICES, dtype=jnp.int32)[:, None]
    owners = jnp.arange(DEVICES, dtype=jnp.int32)[:, None, None, None]

    def forward(node_wide, edge_widened):
        node_blocks = node_wide.reshape(DEVICES, NODE_DEV, D)
        groups = node_blocks[owners, border_list]
        layout = groups.reshape(N_LAT, N_LON, 2, 2, HALO, D).transpose(0, 2, 1, 3, 4, 5)
        layout = layout.reshape(2 * N_LAT, 2 * N_LON, HALO, D)
        layout = jnp.concatenate([layout[:, -1:], layout, layout[:, :1]], 1)
        blank = jnp.zeros((1, 2 * N_LON + 2, HALO, D), jnp.float32).astype(layout.dtype)
        layout = jnp.concatenate([blank, layout, blank], 0)

        def one_device(items):
            device, edge_block, slot_block, receiver_block, active_count = items
            lat_index = (device // N_LON).astype(jnp.int32)
            lon_index = (device % N_LON).astype(jnp.int32)
            zero = jnp.zeros((), jnp.int32)
            cycle = lax.dynamic_slice(layout, (2 * lat_index, 2 * lon_index, zero, zero), (4, 4, HALO, D))
            received = node_blocks[sources, send_list[:, device, :]].reshape(DEVICES * CAP, D)
            table = jnp.concatenate([node_blocks[device], cycle.reshape(16 * HALO, D), received], 0)
            return local_layer(node_blocks[device], table, edge_block, slot_block, receiver_block, active_count, weights)
        results = lax.map(jax.checkpoint(one_device), (jnp.arange(DEVICES, dtype=jnp.int32), edge_widened.reshape(DEVICES, EDGE_PER_SHARD, D), sender_slot.reshape(DEVICES, EDGE_PER_SHARD), receiver.reshape(DEVICES, EDGE_PER_SHARD), edge_count))
        return (results[0].reshape(NODES, D), results[1].reshape(EDGES, D))
    outputs, pull = jax.vjp(forward, node_latent.astype(jnp.float32), edge_latent.astype(jnp.float32))
    node_grad, edge_grad = pull((node_cotangent, edge_cotangent))
    return (outputs[0], outputs[1], node_grad, edge_grad)
```

```python
import functools

import jax
import jax.numpy as jnp
from jax import lax
from jax.experimental import pallas as pl
from jax.experimental.pallas import tpu as pltpu
from jax.sharding import PartitionSpec as P

BF = jnp.bfloat16
F32 = jnp.float32
MESH = pl.DeviceIdType.MESH
N_LAT, N_LON = 8, 16
DEVICES = 128
D = 512
NODE = 256
EDGE = 2048
HALO = 32
CAP = 4
FAR = DEVICES * CAP
BORDER = 16 * HALO
TILE = 256
LIMIT = 56 * 1024 * 1024

def _owner(row):
    return (-1, 1) if row == 0 else (1, 0) if row == 3 else (0, row - 1)


CELLS = []
for _r in range(4):
    for _s in range(4):
        _di, _a = _owner(_r)
        _dj, _b = _owner(_s)
        if _di or _dj:
            CELLS.append((_r * 4 + _s, _di, _dj, _a, _b))


def dot(a, b):
    return jnp.dot(a, b, preferred_element_type=F32)


def dot_t(a, b):
    return lax.dot_general(a, b, (((1,), (1,)), ((), ())), preferred_element_type=F32)


def column(row):
    return jnp.transpose(jnp.broadcast_to(row, (128, 128)))


def onehot_cols(col, base, width):
    lane = lax.broadcasted_iota(jnp.int32, col.shape, 1)
    parts = [
        jnp.where(col == lane + (base + k), 1.0, 0.0).astype(BF) for k in range(0, width, 128)
    ]
    return jnp.concatenate(parts, axis=1)


def onehot_rows(rows, base, height):
    parts = []
    for row in rows:
        place = lax.broadcasted_iota(jnp.int32, (height, 128), 0) + base
        parts.append(jnp.where(place == row, 1.0, 0.0).astype(BF))
    return jnp.concatenate(parts, axis=1) if len(parts) > 1 else parts[0]


def position():
    return lax.axis_index("lat"), lax.axis_index("lon")


def greet(lat, lon):
    me = lat * N_LON + lon
    barrier = pltpu.get_barrier_semaphore()

    def one(step, carry):
        peer = lax.rem(me + step, DEVICES)
        pl.semaphore_signal(
            barrier,
            inc=1,
            device_id=(peer // N_LON, lax.rem(peer, N_LON)),
            device_id_type=MESH,
        )
        return carry

    lax.fori_loop(1, DEVICES, one, 0)
    return barrier


def scatter_far(lat, lon, source, target, send_sem, recv_sem):
    me = lat * N_LON + lon

    def one(step, carry):
        peer = lax.rem(me + step, DEVICES)
        pltpu.make_async_remote_copy(
            src_ref=source.at[peer],
            dst_ref=target.at[me],
            send_sem=send_sem,
            recv_sem=recv_sem,
            device_id=(peer // N_LON, lax.rem(peer, N_LON)),
            device_id_type=MESH,
        ).start()
        return carry

    lax.fori_loop(1, DEVICES, one, 0)


def far_waits(source, target, send_sem, recv_sem):
    some = pl.ds(0, DEVICES - 1)
    pltpu.make_async_copy(source.at[some], target.at[some], recv_sem).wait()
    pltpu.make_async_copy(source.at[some], target.at[some], send_sem).wait()


def around(lat, lon, di, dj):
    return (lax.rem(lat + di + N_LAT, N_LAT), lax.rem(lon + dj + N_LON, N_LON))


def fetch_kernel(
    node, slots, groups, border, far, wide, out, send_sem, recv_sem, own_sem, cell_send, cell_recv
):
    lat, lon = position()
    me = lat * N_LON + lon
    barrier = greet(lat, lon)
    rows = dot(onehot_cols(column(groups[...]), 0, NODE), node[...]).astype(BF)
    for a in range(2):
        for b in range(2):
            g = 2 * a + b
            border[(a + 1) * 4 + b + 1] = rows[g * HALO : (g + 1) * HALO]
    for block in range(FAR // 128):
        rows = dot(onehot_cols(column(slots[block : block + 1, :]), 0, NODE), node[...])
        for k in range(4):
            wide[pl.ds(512 * block + k, 128, stride=4), :] = rows[:, 128 * k : 128 * k + 128]
    out[...] = wide[...].astype(BF).reshape(DEVICES, 16, 128)
    pl.semaphore_wait(barrier, DEVICES - 1)
    copies = []
    for i, (cell, di, dj, a, b) in enumerate(CELLS):
        copy = pltpu.make_async_remote_copy(
            src_ref=border.at[(a + 1) * 4 + b + 1],
            dst_ref=border.at[cell],
            send_sem=cell_send.at[i],
            recv_sem=cell_recv.at[i],
            device_id=around(lat, lon, -di, -dj),
            device_id_type=MESH,
        )
        copy.start()
        copies.append(copy)
    scatter_far(lat, lon, out, far, send_sem, recv_sem)
    own = pltpu.make_async_copy(out.at[me], far.at[me], own_sem)
    own.start()
    own.wait()
    for copy in copies:
        copy.wait()
    far_waits(out, far, send_sem, recv_sem)


def return_kernel(
    partial, border_grad, far_grad, slots, groups, total,
    cells, far, wide, send_sem, recv_sem, own_sem, cell_send, cell_recv
):
    lat, lon = position()
    me = lat * N_LON + lon
    barrier = greet(lat, lon)
    pl.semaphore_wait(barrier, DEVICES - 1)
    copies = []
    for i, (cell, di, dj, a, b) in enumerate(CELLS):
        kind = 2 * abs(di) + abs(dj) - 1
        copy = pltpu.make_async_remote_copy(
            src_ref=border_grad.at[cell],
            dst_ref=cells.at[kind * 4 + 2 * a + b],
            send_sem=cell_send.at[i],
            recv_sem=cell_recv.at[i],
            device_id=around(lat, lon, di, dj),
            device_id_type=MESH,
        )
        copy.start()
        copies.append(copy)
    scatter_far(lat, lon, far_grad, far, send_sem, recv_sem)
    own = pltpu.make_async_copy(far_grad.at[me], far.at[me], own_sem)
    own.start()
    own.wait()
    for copy in copies:
        copy.wait()
    picked = onehot_rows([groups[...]], 0, NODE)
    summed = partial[...]
    for kind in range(3):
        summed = summed + dot(picked, cells[4 * kind : 4 * kind + 4].reshape(128, D))
    far_waits(far_grad, far, send_sem, recv_sem)
    wide[...] = far[...].reshape(FAR * 4, 128).astype(F32)
    returned = jnp.concatenate(
        [wide[pl.ds(k, FAR, stride=4), :].astype(BF) for k in range(4)], axis=1
    )
    lists = onehot_rows([slots[i : i + 1, :] for i in range(FAR // 128)], 0, NODE)
    total[...] = summed + dot(lists, returned)


def silu_parts(pre):
    sig = 1.0 / (1.0 + jnp.exp(-pre))
    value = pre * sig
    return value, sig + value * (1.0 - sig)


def normal(values):
    mean = jnp.mean(values, -1, keepdims=True)
    centred = values - mean
    var = jnp.mean(centred * centred, -1, keepdims=True)
    return centred, lax.rsqrt(var + 1e-05)


def layer_kernel(
    count, sender, receiver, groups, node, border, far, node_cot,
    hidden_bias, message_bias, edge_scales, node_bias, update_bias, node_scales,
    edge_h, cot_h, we_h, ws_h, wr_h, wm_h, wself_h, wsum_h, wu_h,
    edge_out_h, grad_out_h, node_out, partial, border_grad, far_grad,
    edge, cot, we, ws, wr, wm, wself, wsum, wu,
    edge_out, grad_out, wide, table, rproj, scol, rcol, xhat, slope, message, dpre, rstd, dsummed,
    in_sems, out_sems, grad_sems,
):
    loads = {}
    for i, (name, src, dst) in enumerate(
        (
            ("ws", ws_h, ws), ("wr", wr_h, wr), ("we", we_h, we), ("edge", edge_h, edge),
            ("wm", wm_h, wm), ("wself", wself_h, wself), ("wsum", wsum_h, wsum),
            ("wu", wu_h, wu), ("cot", cot_h, cot),
        )
    ):
        loads[name] = pltpu.make_async_copy(src, dst, in_sems.at[i])
        loads[name].start()
    for j in range(EDGE // 128):
        at = pl.ds(128 * j, 128)
        scol[at, :] = column(sender[j : j + 1, :])
        rcol[at, :] = column(receiver[j : j + 1, :])
    wide[...] = far[...].reshape(FAR * 4, 128).astype(F32)
    loads["ws"].wait()
    table[0:NODE] = dot(node[...], ws[...]).astype(BF)
    for h in range(2):
        at = pl.ds(NODE + 256 * h, 256)
        table[at] = dot(border[8 * h : 8 * h + 8].reshape(256, D), ws[...]).astype(BF)
    for h in range(2):
        rows = jnp.concatenate(
            [wide[pl.ds(1024 * h + k, 256, stride=4), :].astype(BF) for k in range(4)], axis=1
        )
        table[pl.ds(NODE + BORDER + 256 * h, 256)] = dot(rows, ws[...]).astype(BF)
    loads["wr"].wait()
    rproj[...] = (dot(node[...], wr[...]) + hidden_bias[...]).astype(BF)
    loads["we"].wait()
    loads["edge"].wait()
    loads["wm"].wait()
    live_edges = count[0]

    def forward(i, carry):
        at = pl.ds(pl.multiple_of(i * TILE, TILE), TILE)
        pre = (
            dot(edge[at, :], we[...])
            + dot(onehot_cols(scol[at, :], 0, NODE + BORDER + FAR), table[...])
            + dot(onehot_cols(rcol[at, :], 0, NODE), rproj[...])
        )
        value, grad = silu_parts(pre)
        slope[at, :] = grad.astype(BF)
        centred, scale = normal(dot(value.astype(BF), wm[...]) + message_bias[...])
        place = lax.broadcasted_iota(jnp.int32, (TILE, 1), 0) + i * TILE
        scale = jnp.where(place < live_edges, scale, 0.0)
        rstd[at, :] = scale
        hat = centred * scale
        xhat[at, :] = hat.astype(BF)
        said = hat * edge_scales[...]
        message[at, :] = said.astype(BF)
        edge_out[at, :] = (edge[at, :].astype(F32) + said).astype(BF)
        pltpu.make_async_copy(edge_out.at[at, :], edge_out_h.at[at, :], out_sems.at[i]).start()
        return carry

    lax.fori_loop(0, EDGE // TILE, forward, 0)

    receivers = [receiver[j : j + 1, :] for j in range(EDGE // 128)]
    summed = dot(onehot_rows(receivers, 0, NODE), message[...]).astype(BF)
    loads["wself"].wait()
    loads["wsum"].wait()
    value, grad = silu_parts(
        dot(node[...], wself[...]) + dot(summed, wsum[...]) + node_bias[...]
    )
    loads["wu"].wait()
    centred, scale = normal(dot(value.astype(BF), wu[...]) + update_bias[...])
    hat = centred * scale
    node_out[...] = (node[...].astype(F32) + hat * node_scales[...]).astype(BF)
    upper = node_cot[...].astype(F32)
    g = upper * node_scales[...]
    back = scale * (
        g - jnp.mean(g, -1, keepdims=True) - hat * jnp.mean(g * hat, -1, keepdims=True)
    )
    inner = (dot_t(back.astype(BF), wu[...]) * grad).astype(BF)
    dsummed[...] = dot_t(inner, wsum[...]).astype(BF)
    partial[...] = upper + dot_t(inner, wself[...])
    loads["cot"].wait()

    def backward(i, carry):
        at = pl.ds(pl.multiple_of(i * TILE, TILE), TILE)
        upper = cot[at, :].astype(F32)
        g = (upper + dot(onehot_cols(rcol[at, :], 0, NODE), dsummed[...])) * edge_scales[...]
        hat = xhat[at, :].astype(F32)
        back = rstd[at, :] * (
            g - jnp.mean(g, -1, keepdims=True) - hat * jnp.mean(g * hat, -1, keepdims=True)
        )
        inner = (dot_t(back.astype(BF), wm[...]) * slope[at, :].astype(F32)).astype(BF)
        dpre[at, :] = inner
        grad_out[at, :] = upper + dot_t(inner, we[...])
        pltpu.make_async_copy(grad_out.at[at, :], grad_out_h.at[at, :], grad_sems.at[i]).start()
        return carry

    lax.fori_loop(0, EDGE // TILE, backward, 0)

    senders = [sender[j : j + 1, :] for j in range(EDGE // 128)]

    def table_grad(base):
        rows = dot(onehot_rows(senders, base, 256), dpre[...]).astype(BF)
        return dot_t(rows, ws[...])

    for h in range(2):
        rows = table_grad(NODE + BORDER + 256 * h)
        for k in range(4):
            wide[pl.ds(1024 * h + k, 256, stride=4), :] = rows[:, 128 * k : 128 * k + 128]
    far_grad[...] = wide[...].astype(BF).reshape(DEVICES, 16, 128)
    for h in range(2):
        border_grad[8 * h : 8 * h + 8] = table_grad(NODE + 256 * h).astype(BF).reshape(8, HALO, D)
    center = jnp.concatenate([border_grad[cell] for cell in (5, 6, 9, 10)], axis=0)
    received = dot(onehot_rows(receivers, 0, NODE), dpre[...]).astype(BF)
    partial[...] += (
        table_grad(0)
        + dot_t(received, wr[...])
        + dot(onehot_rows([groups[...]], 0, NODE), center)
    )
    for i in range(EDGE // TILE):
        at = pl.ds(i * TILE, TILE)
        pltpu.make_async_copy(edge_out.at[at, :], edge_out_h.at[at, :], out_sems.at[i]).wait()
        pltpu.make_async_copy(grad_out.at[at, :], grad_out_h.at[at, :], grad_sems.at[i]).wait()


def vmem(count):
    return [pl.BlockSpec(memory_space=pltpu.VMEM)] * count


def per_device(
    node_latent, edge_latent, sender_slot, receiver, border_list, send_list, edge_count,
    edge_weight, sender_weight, receiver_weight, hidden_bias, message_weight, message_bias,
    edge_scales, self_weight, summed_weight, node_bias, update_weight, update_bias, node_scales,
    node_cotangent, edge_cotangent,
):
    groups = border_list.reshape(1, 4 * HALO)
    slots = send_list.reshape(FAR // 128, 128)
    sems = pltpu.SemaphoreType.DMA
    chunks = jax.ShapeDtypeStruct((DEVICES, 16, 128), BF)
    cells = jax.ShapeDtypeStruct((16, HALO, D), BF)
    border, far = pl.pallas_call(
        fetch_kernel,
        out_shape=(cells, chunks),
        in_specs=vmem(3),
        out_specs=tuple(vmem(2)),
        scratch_shapes=[
            pltpu.VMEM((FAR * 4, 128), F32),
            pltpu.VMEM((DEVICES, 16, 128), BF),
            sems, sems, sems, sems((12,)), sems((12,)),
        ],
        compiler_params=pltpu.CompilerParams(
            collective_id=0, has_side_effects=True, vmem_limit_bytes=LIMIT
        ),
        name="fetch",
    )(node_latent, slots, groups)

    weight = pltpu.VMEM((D, D), BF)
    half = pltpu.VMEM((EDGE, D), BF)
    any_space = pl.BlockSpec(memory_space=pl.ANY)
    vector = lambda v: v.reshape(1, D)
    edge_result, edge_grad, node_result, partial, border_grad, far_grad = pl.pallas_call(
        layer_kernel,
        out_shape=(
            jax.ShapeDtypeStruct((EDGE, D), BF),
            jax.ShapeDtypeStruct((EDGE, D), F32),
            jax.ShapeDtypeStruct((NODE, D), BF),
            jax.ShapeDtypeStruct((NODE, D), F32),
            cells,
            chunks,
        ),
        in_specs=[pl.BlockSpec(memory_space=pltpu.SMEM)] + vmem(13) + [any_space] * 9,
        out_specs=tuple([any_space] * 2 + vmem(4)),
        scratch_shapes=[half, half]
        + [weight] * 7
        + [
            half,
            pltpu.VMEM((EDGE, D), F32),
            pltpu.VMEM((FAR * 4, 128), F32),
            pltpu.VMEM((NODE + BORDER + FAR, D), BF),
            pltpu.VMEM((NODE, D), BF),
            pltpu.VMEM((EDGE, 128), jnp.int32),
            pltpu.VMEM((EDGE, 128), jnp.int32),
            half, half, half, half,
            pltpu.VMEM((EDGE, 1), F32),
            pltpu.VMEM((NODE, D), BF),
            sems((9,)),
            sems((EDGE // TILE,)),
            sems((EDGE // TILE,)),
        ],
        compiler_params=pltpu.CompilerParams(vmem_limit_bytes=LIMIT),
        name="layer",
    )(
        edge_count, sender_slot.reshape(EDGE // 128, 128), receiver.reshape(EDGE // 128, 128),
        groups, node_latent, border, far, node_cotangent,
        vector(hidden_bias), vector(message_bias), vector(edge_scales),
        vector(node_bias), vector(update_bias), vector(node_scales),
        edge_latent, edge_cotangent, edge_weight, sender_weight, receiver_weight,
        message_weight, self_weight, summed_weight, update_weight,
    )

    node_grad = pl.pallas_call(
        return_kernel,
        out_shape=jax.ShapeDtypeStruct((NODE, D), F32),
        in_specs=vmem(5),
        out_specs=vmem(1)[0],
        scratch_shapes=[
            pltpu.VMEM((12, HALO, D), BF),
            pltpu.VMEM((DEVICES, 16, 128), BF),
            pltpu.VMEM((FAR * 4, 128), F32),
            sems, sems, sems, sems((12,)), sems((12,)),
        ],
        compiler_params=pltpu.CompilerParams(
            collective_id=1, has_side_effects=True, vmem_limit_bytes=LIMIT
        ),
        name="give_back",
    )(partial, border_grad, far_grad, slots, groups)
    return node_result, edge_result, node_grad, edge_grad


def solution(mesh):
    both = ("lat", "lon")
    placed = (
        P(both, None), P(both, None), P(both), P(both), P(both, None, None, None),
        P(both, None, None), P(both),
        P(), P(), P(), P(), P(), P(), P(), P(), P(), P(), P(), P(), P(),
        P(both, None), P(both, None),
    )
    return jax.shard_map(
        per_device,
        mesh=mesh,
        in_specs=placed,
        out_specs=(P(both, None),) * 4,
        check_vma=False,
    )
```

```python
import functools

import jax
import jax.numpy as jnp
from jax import lax
from jax.experimental import pallas as pl
from jax.experimental.pallas import tpu as pltpu
from jax.sharding import PartitionSpec as P

BF = jnp.bfloat16
F32 = jnp.float32
MESH = pl.DeviceIdType.MESH
N_LAT, N_LON = 8, 16
DEVICES = 128
D = 512
NODE = 256
EDGE = 2048
HALO = 32
CAP = 4
FAR = DEVICES * CAP
BORDER = 16 * HALO
TILE = 512
LIMIT = 44 * 1024 * 1024

def _owner(row):
    return (-1, 1) if row == 0 else (1, 0) if row == 3 else (0, row - 1)


CELLS = []
for _r in range(4):
    for _s in range(4):
        _di, _a = _owner(_r)
        _dj, _b = _owner(_s)
        if _di or _dj:
            CELLS.append((_r * 4 + _s, _di, _dj, _a, _b))


def dot(a, b):
    return jnp.dot(a, b, preferred_element_type=F32)


def dot_t(a, b):
    return lax.dot_general(a, b, (((1,), (1,)), ((), ())), preferred_element_type=F32)


def column(row):
    return jnp.transpose(jnp.broadcast_to(row, (128, 128)))


def onehot_cols(col, base, width):
    lane = lax.broadcasted_iota(jnp.int32, col.shape, 1)
    parts = [
        jnp.where(col == lane + (base + k), 1.0, 0.0).astype(BF) for k in range(0, width, 128)
    ]
    return jnp.concatenate(parts, axis=1)


def onehot_rows(rows, base, height):
    parts = []
    for row in rows:
        place = lax.broadcasted_iota(jnp.int32, (height, 128), 0) + base
        parts.append(jnp.where(place == row, 1.0, 0.0).astype(BF))
    return jnp.concatenate(parts, axis=1) if len(parts) > 1 else parts[0]


def position():
    return lax.axis_index("lat"), lax.axis_index("lon")


def greet(lat, lon):
    me = lat * N_LON + lon
    barrier = pltpu.get_barrier_semaphore()

    def one(step, carry):
        peer = lax.rem(me + step, DEVICES)
        pl.semaphore_signal(
            barrier,
            inc=1,
            device_id=(peer // N_LON, lax.rem(peer, N_LON)),
            device_id_type=MESH,
        )
        return carry

    lax.fori_loop(1, DEVICES, one, 0)
    return barrier


def scatter_far(lat, lon, source, target, send_sem, recv_sem):
    me = lat * N_LON + lon

    def one(step, carry):
        peer = lax.rem(me + step, DEVICES)
        pltpu.make_async_remote_copy(
            src_ref=source.at[peer],
            dst_ref=target.at[me],
            send_sem=send_sem,
            recv_sem=recv_sem,
            device_id=(peer // N_LON, lax.rem(peer, N_LON)),
            device_id_type=MESH,
        ).start()
        return carry

    lax.fori_loop(1, DEVICES, one, 0)


def far_waits(source, target, send_sem, recv_sem):
    some = pl.ds(0, DEVICES - 1)
    pltpu.make_async_copy(source.at[some], target.at[some], recv_sem).wait()
    pltpu.make_async_copy(source.at[some], target.at[some], send_sem).wait()


def around(lat, lon, di, dj):
    return (lax.rem(lat + di + N_LAT, N_LAT), lax.rem(lon + dj + N_LON, N_LON))


def group_row(groups):
    return jnp.concatenate([groups[0, a, b : b + 1, :] for a in range(2) for b in range(2)], axis=1)


def columns(rows, target):
    for j in range(EDGE // 128):
        target[128 * j : 128 * j + 128, :] = column(rows[j : j + 1, :])


def silu_parts(pre):
    sig = 1.0 / (1.0 + jnp.exp(-pre))
    value = pre * sig
    return value, sig + value * (1.0 - sig)


def normal(values):
    mean = jnp.mean(values, -1, keepdims=True)
    centred = values - mean
    var = jnp.mean(centred * centred, -1, keepdims=True)
    return centred, lax.rsqrt(var + 1e-05)


def send_cells(lat, lon, source, target, inward, cell_send, cell_recv):
    copies = []
    for i, (cell, di, dj, a, b) in enumerate(CELLS):
        if inward:
            kind = 2 * abs(di) + abs(dj) - 1
            src, dst, peer = source.at[cell], target.at[kind * 4 + 2 * a + b], (di, dj)
        else:
            src, dst, peer = source.at[(a + 1) * 4 + b + 1], target.at[cell], (-di, -dj)
        copy = pltpu.make_async_remote_copy(
            src_ref=src,
            dst_ref=dst,
            send_sem=cell_send.at[i],
            recv_sem=cell_recv.at[i],
            device_id=around(lat, lon, *peer),
            device_id_type=MESH,
        )
        copy.start()
        copies.append(copy)
    return copies


def layer_kernel(
    count, node_h, groups_h, slots_h, ws_h, wr_h, hidden_bias_h, sender_h, receiver_h, we_h, edge_h,
    wm_h, message_bias_h, edge_scales_h, wself_h, wsum_h, node_bias_h, wu_h, update_bias_h,
    node_scales_h, node_cot_h, cot_h,
    edge_out_h, dpre_h, node_out_h, total_h,
    node, groups, slots, ws, wr, hidden_bias, sender, receiver, we, edge,
    wm, message_bias, edge_scales, wself, wsum, node_bias, wu, update_bias,
    node_scales, node_cot, cot,
    border, wide, out, far, table, rproj, scol, rcol, pre,
    edge_out, xhat, slope, message, dpre, rstd, dsummed, node_out, total,
    border_grad, far_grad, far_back, cells_back,
    in_sems, edge_sems, dpre_sems, node_sems, far_sems, cell_send, cell_recv, back_send, back_recv,
):
    lat, lon = position()
    me = lat * N_LON + lon
    loads = []
    for i, (src, dst) in enumerate(
        (
            (node_h, node), (groups_h, groups), (slots_h, slots), (ws_h, ws), (wr_h, wr),
            (hidden_bias_h, hidden_bias), (sender_h, sender), (receiver_h, receiver),
            (we_h, we), (edge_h, edge), (wm_h, wm), (message_bias_h, message_bias),
            (edge_scales_h, edge_scales), (wself_h, wself), (wsum_h, wsum),
            (node_bias_h, node_bias), (wu_h, wu), (update_bias_h, update_bias),
            (node_scales_h, node_scales), (node_cot_h, node_cot), (cot_h, cot),
        )
    ):
        load = pltpu.make_async_copy(src, dst, in_sems.at[i])
        load.start()
        loads.append(load)
    barrier = greet(lat, lon)

    def arrived(first, last):
        for load in loads[first:last]:
            load.wait()

    arrived(0, 3)
    rows = dot(onehot_cols(column(group_row(groups)), 0, NODE), node[...]).astype(BF)
    for a in range(2):
        for b in range(2):
            g = 2 * a + b
            border[(a + 1) * 4 + b + 1] = rows[g * HALO : (g + 1) * HALO]
    for c in range(CAP):
        rows = dot(onehot_cols(column(slots[0, c : c + 1, :]), 0, NODE), node[...])
        for k in range(4):
            wide[pl.ds(4 * c + k, DEVICES, stride=16), :] = rows[:, 128 * k : 128 * k + 128]
    out[...] = wide[...].astype(BF).reshape(DEVICES, 16, 128)
    pl.semaphore_wait(barrier, DEVICES - 1)
    copies = send_cells(lat, lon, border, border, False, cell_send, cell_recv)
    scatter_far(lat, lon, out, far, far_sems.at[0], far_sems.at[1])
    own = pltpu.make_async_copy(out.at[me], far.at[me], far_sems.at[2])
    own.start()
    arrived(3, 10)
    columns(sender, scol)
    columns(receiver, rcol)
    table[0:NODE] = dot(node[...], ws[...]).astype(BF)
    rproj[...] = (dot(node[...], wr[...]) + hidden_bias[...]).astype(BF)
    for copy in copies:
        copy.wait()
    for h in range(2):
        at = pl.ds(NODE + 256 * h, 256)
        table[at] = dot(border[8 * h : 8 * h + 8].reshape(256, D), ws[...]).astype(BF)

    def near(i, carry):
        at = pl.ds(pl.multiple_of(i * TILE, TILE), TILE)
        pre[at, :] = (
            dot(edge[at, :], we[...])
            + dot(onehot_cols(scol[at, :], 0, NODE + BORDER), table[0 : NODE + BORDER])
            + dot(onehot_cols(rcol[at, :], 0, NODE), rproj[...])
        )
        return carry

    lax.fori_loop(0, EDGE // TILE, near, 0)
    arrived(10, 21)
    own.wait()
    far_waits(out, far, far_sems.at[0], far_sems.at[1])
    wide[...] = far[...].reshape(FAR * 4, 128).astype(F32)
    for h in range(2):
        rows = jnp.concatenate(
            [wide[pl.ds(1024 * h + k, 256, stride=4), :].astype(BF) for k in range(4)], axis=1
        )
        table[pl.ds(NODE + BORDER + 256 * h, 256)] = dot(rows, ws[...]).astype(BF)
    live_edges = count[0]

    def forward(i, carry):
        at = pl.ds(pl.multiple_of(i * TILE, TILE), TILE)
        value, grad = silu_parts(
            pre[at, :]
            + dot(
                onehot_cols(scol[at, :], NODE + BORDER, FAR),
                table[NODE + BORDER : NODE + BORDER + FAR],
            )
        )
        slope[at, :] = grad.astype(BF)
        centred, scale = normal(dot(value.astype(BF), wm[...]) + message_bias[...])
        place = lax.broadcasted_iota(jnp.int32, (TILE, 1), 0) + i * TILE
        scale = jnp.where(place < live_edges, scale, 0.0)
        rstd[at, :] = scale
        hat = centred * scale
        xhat[at, :] = hat.astype(BF)
        said = hat * edge_scales[...]
        message[at, :] = said.astype(BF)
        edge_out[at, :] = (edge[at, :].astype(F32) + said).astype(BF)
        pltpu.make_async_copy(edge_out.at[at, :], edge_out_h.at[at, :], edge_sems.at[i]).start()
        return carry

    lax.fori_loop(0, EDGE // TILE, forward, 0)

    receivers = [receiver[j : j + 1, :] for j in range(EDGE // 128)]
    summed = dot(onehot_rows(receivers, 0, NODE), message[...]).astype(BF)
    value, grad = silu_parts(
        dot(node[...], wself[...]) + dot(summed, wsum[...]) + node_bias[...]
    )
    centred, scale = normal(dot(value.astype(BF), wu[...]) + update_bias[...])
    hat = centred * scale
    node_out[...] = (node[...].astype(F32) + hat * node_scales[...]).astype(BF)
    node_copy = pltpu.make_async_copy(node_out, node_out_h, node_sems.at[0])
    node_copy.start()
    upper = node_cot[...].astype(F32)
    g = upper * node_scales[...]
    back = scale * (
        g - jnp.mean(g, -1, keepdims=True) - hat * jnp.mean(g * hat, -1, keepdims=True)
    )
    inner = (dot_t(back.astype(BF), wu[...]) * grad).astype(BF)
    dsummed[...] = dot_t(inner, wsum[...]).astype(BF)
    total[...] = upper + dot_t(inner, wself[...])

    def backward(i, carry):
        at = pl.ds(pl.multiple_of(i * TILE, TILE), TILE)
        upper = cot[at, :].astype(F32)
        g = (upper + dot(onehot_cols(rcol[at, :], 0, NODE), dsummed[...])) * edge_scales[...]
        hat = xhat[at, :].astype(F32)
        back = rstd[at, :] * (
            g - jnp.mean(g, -1, keepdims=True) - hat * jnp.mean(g * hat, -1, keepdims=True)
        )
        dpre[at, :] = (dot_t(back.astype(BF), wm[...]) * slope[at, :].astype(F32)).astype(BF)
        pltpu.make_async_copy(dpre.at[at, :], dpre_h.at[at, :], dpre_sems.at[i]).start()
        return carry

    lax.fori_loop(0, EDGE // TILE, backward, 0)

    senders = [sender[j : j + 1, :] for j in range(EDGE // 128)]

    def table_grad(base):
        rows = dot(onehot_rows(senders, base, 256), dpre[...]).astype(BF)
        return dot_t(rows, ws[...])

    for h in range(2):
        rows = table_grad(NODE + BORDER + 256 * h)
        for k in range(4):
            wide[pl.ds(1024 * h + k, 256, stride=4), :] = rows[:, 128 * k : 128 * k + 128]
    far_grad[...] = wide[...].astype(BF).reshape(DEVICES, 16, 128)
    scatter_far(lat, lon, far_grad, far_back, far_sems.at[3], far_sems.at[4])
    own = pltpu.make_async_copy(far_grad.at[me], far_back.at[me], far_sems.at[5])
    own.start()
    for h in range(2):
        border_grad[8 * h : 8 * h + 8] = table_grad(NODE + 256 * h).astype(BF).reshape(8, HALO, D)
    copies = send_cells(lat, lon, border_grad, cells_back, True, back_send, back_recv)
    received = dot(onehot_rows(receivers, 0, NODE), dpre[...]).astype(BF)
    picked = onehot_rows([group_row(groups)], 0, NODE)
    center = jnp.concatenate([border_grad[cell] for cell in (5, 6, 9, 10)], axis=0)
    total[...] += table_grad(0) + dot_t(received, wr[...]) + dot(picked, center)
    for copy in copies:
        copy.wait()
    summed = dot(picked, cells_back[0:4].reshape(128, D))
    for kind in (1, 2):
        summed = summed + dot(picked, cells_back[4 * kind : 4 * kind + 4].reshape(128, D))
    total[...] += summed
    own.wait()
    far_waits(far_grad, far_back, far_sems.at[3], far_sems.at[4])
    wide[...] = far_back[...].reshape(FAR * 4, 128).astype(F32)
    returned = jnp.concatenate(
        [
            jnp.concatenate(
                [wide[pl.ds(4 * c + k, DEVICES, stride=16), :].astype(BF) for k in range(4)], axis=1
            )
            for c in range(CAP)
        ],
        axis=0,
    )
    lists = onehot_rows([slots[0, c : c + 1, :] for c in range(CAP)], 0, NODE)
    total[...] += dot(lists, returned)
    total_copy = pltpu.make_async_copy(total, total_h, node_sems.at[1])
    total_copy.start()
    for i in range(EDGE // TILE):
        at = pl.ds(i * TILE, TILE)
        pltpu.make_async_copy(edge_out.at[at, :], edge_out_h.at[at, :], edge_sems.at[i]).wait()
        pltpu.make_async_copy(dpre.at[at, :], dpre_h.at[at, :], dpre_sems.at[i]).wait()
    node_copy.wait()
    total_copy.wait()


def finish_kernel(
    edge_i, node_i, total_i, dpre_h, cot_h, we_h, edge_o, node_o, total_o, grad_o,
    dpre, cot, we, grad, pass_sems, we_sem, dpre_sems, cot_sems, grad_sems,
):
    weight = pltpu.make_async_copy(we_h, we, we_sem)
    weight.start()
    tiles = [pl.ds(i * TILE, TILE) for i in range(EDGE // TILE)]
    loads = []
    for i, at in enumerate(tiles):
        pair = (
            pltpu.make_async_copy(dpre_h.at[at, :], dpre.at[at, :], dpre_sems.at[i]),
            pltpu.make_async_copy(cot_h.at[at, :], cot.at[at, :], cot_sems.at[i]),
        )
        for copy in pair:
            copy.start()
        loads.append(pair)
    passed = [
        pltpu.make_async_copy(src, dst, pass_sems.at[i])
        for i, (src, dst) in enumerate(((edge_i, edge_o), (node_i, node_o), (total_i, total_o)))
    ]
    for copy in passed:
        copy.start()
    weight.wait()
    stores = []
    for i, at in enumerate(tiles):
        for copy in loads[i]:
            copy.wait()
        grad[at, :] = cot[at, :].astype(F32) + dot_t(dpre[at, :], we[...])
        store = pltpu.make_async_copy(grad.at[at, :], grad_o.at[at, :], grad_sems.at[i])
        store.start()
        stores.append(store)
    for copy in passed + stores:
        copy.wait()


def vmem(count):
    return [pl.BlockSpec(memory_space=pltpu.VMEM)] * count


def per_device(
    node_latent, edge_latent, sender_slot, receiver, border_list, send_list, edge_count,
    edge_weight, sender_weight, receiver_weight, hidden_bias, message_weight, message_bias,
    edge_scales, self_weight, summed_weight, node_bias, update_weight, update_bias, node_scales,
    node_cotangent, edge_cotangent,
):
    slots = send_list.transpose(0, 2, 1)
    sender = sender_slot.reshape(EDGE // 128, 128)
    receiver = receiver.reshape(EDGE // 128, 128)
    sems = pltpu.SemaphoreType.DMA
    tiles = sems((EDGE // TILE,))
    cells = pltpu.VMEM((16, HALO, D), BF)
    chunk = pltpu.VMEM((DEVICES, 16, 128), BF)
    wide = pltpu.VMEM((FAR * 4, 128), F32)
    weight = pltpu.VMEM((D, D), BF)
    half = pltpu.VMEM((EDGE, D), BF)
    full = pltpu.VMEM((EDGE, D), F32)
    nodes = pltpu.VMEM((NODE, D), BF)
    column_of = pltpu.VMEM((EDGE, 128), jnp.int32)
    any_space = pl.BlockSpec(memory_space=pl.ANY)
    hbm = pl.BlockSpec(memory_space=pltpu.HBM)
    line = pltpu.VMEM((1, D), F32)
    slot_rows = pltpu.VMEM((EDGE // 128, 128), jnp.int32)
    keep = lambda v: pltpu.with_memory_space_constraint(v, pltpu.HBM)
    vector = lambda v: v.reshape(1, D)
    results = (
        jax.ShapeDtypeStruct((EDGE, D), BF),
        jax.ShapeDtypeStruct((NODE, D), BF),
        jax.ShapeDtypeStruct((NODE, D), F32),
    )
    edges = jax.ShapeDtypeStruct((EDGE, D), BF)
    edge_result, dpre, node_result, node_grad = pl.pallas_call(
        layer_kernel,
        out_shape=(results[0], edges, results[1], results[2]),
        in_specs=[pl.BlockSpec(memory_space=pltpu.SMEM)] + [hbm] * 21,
        out_specs=(any_space,) * 4,
        scratch_shapes=[
            nodes, pltpu.VMEM((1, 2, 2, HALO), jnp.int32), pltpu.VMEM((1, CAP, DEVICES), jnp.int32),
            weight, weight, line, slot_rows, slot_rows, weight, half,
            weight, line, line, weight, weight, line, weight, line, line, nodes, half,
        ]
        + [
            cells, wide, chunk, chunk, pltpu.VMEM((NODE + BORDER + FAR, D), BF), nodes,
            column_of, column_of, full,
            half, half, half, half, half, pltpu.VMEM((EDGE, 1), F32), nodes, nodes,
            pltpu.VMEM((NODE, D), F32),
            cells, chunk, chunk, pltpu.VMEM((12, HALO, D), BF),
            sems((21,)), tiles, tiles, sems((2,)), sems((6,)),
            sems((12,)), sems((12,)), sems((12,)), sems((12,)),
        ],
        compiler_params=pltpu.CompilerParams(
            collective_id=0, has_side_effects=True, vmem_limit_bytes=LIMIT
        ),
        name="layer",
    )(
        edge_count,
        *map(keep, (
        node_latent, border_list, slots, sender_weight, receiver_weight,
        vector(hidden_bias), sender, receiver, edge_weight, edge_latent,
        message_weight, vector(message_bias), vector(edge_scales), self_weight, summed_weight,
        vector(node_bias), update_weight, vector(update_bias), vector(node_scales),
        node_cotangent, edge_cotangent,
        )),
    )
    edge_result, node_result, node_grad, edge_grad = pl.pallas_call(
        finish_kernel,
        out_shape=(*results, jax.ShapeDtypeStruct((EDGE, D), F32)),
        in_specs=[any_space] * 4 + [hbm] * 2,
        out_specs=(any_space,) * 4,
        scratch_shapes=[half, half, weight, full, sems((3,)), sems, tiles, tiles, tiles],
        compiler_params=pltpu.CompilerParams(vmem_limit_bytes=16 * 1024 * 1024),
        name="finish",
    )(edge_result, node_result, node_grad, dpre, keep(edge_cotangent), keep(edge_weight))
    return node_result, edge_result, node_grad, edge_grad


def solution(mesh):
    both = ("lat", "lon")
    placed = (
        P(both, None), P(both, None), P(both), P(both), P(both, None, None, None),
        P(both, None, None), P(both),
        P(), P(), P(), P(), P(), P(), P(), P(), P(), P(), P(), P(), P(),
        P(both, None), P(both, None),
    )
    return jax.shard_map(
        per_device,
        mesh=mesh,
        in_specs=placed,
        out_specs=(P(both, None),) * 4,
        check_vma=False,
    )
```

```python
import functools

import jax
import jax.numpy as jnp
from jax import lax
from jax.experimental import pallas as pl
from jax.experimental.pallas import tpu as pltpu
from jax.sharding import PartitionSpec as P

BF = jnp.bfloat16
F32 = jnp.float32
MESH = pl.DeviceIdType.MESH
N_LAT, N_LON = 8, 16
DEVICES = 128
D = 512
NODE = 256
EDGE = 2048
HALO = 32
CAP = 4
FAR = DEVICES * CAP
BORDER = 16 * HALO
TILE = 1024
LIMIT = 46 * 1024 * 1024
OUTER = NODE + 4 * HALO
REMOTE = 12 * HALO + FAR

def _owner(row):
    return (-1, 1) if row == 0 else (1, 0) if row == 3 else (0, row - 1)


CELLS = []
for _r in range(4):
    for _s in range(4):
        _di, _a = _owner(_r)
        _dj, _b = _owner(_s)
        if _di or _dj:
            CELLS.append((_r * 4 + _s, _di, _dj, _a, _b))


def dot(a, b):
    return jnp.dot(a, b, preferred_element_type=F32)


def dot_t(a, b):
    return lax.dot_general(a, b, (((1,), (1,)), ((), ())), preferred_element_type=F32)


def column(row):
    return jnp.transpose(jnp.broadcast_to(row, (128, 128)))


def onehot_cols(col, base, width):
    lane = lax.broadcasted_iota(jnp.int32, col.shape, 1)
    parts = [
        jnp.where(col == lane + (base + k), 1.0, 0.0).astype(BF) for k in range(0, width, 128)
    ]
    return jnp.concatenate(parts, axis=1)


def onehot_rows(rows, base, height):
    parts = []
    for row in rows:
        place = lax.broadcasted_iota(jnp.int32, (height, 128), 0) + base
        parts.append(jnp.where(place == row, 1.0, 0.0).astype(BF))
    return jnp.concatenate(parts, axis=1) if len(parts) > 1 else parts[0]


def position():
    return lax.axis_index("lat"), lax.axis_index("lon")


def greet(lat, lon):
    barrier = pltpu.get_barrier_semaphore()
    lats = [lax.rem(lat + i, N_LAT) for i in range(N_LAT)]
    lons = [lax.rem(lon + j, N_LON) for j in range(N_LON)]
    for j in range(N_LON):
        for i in range(N_LAT):
            if i or j:
                pl.semaphore_signal(
                    barrier, inc=1, device_id=(lats[i], lons[j]), device_id_type=MESH
                )
    return barrier


def sender_place(slot):
    place = jnp.where(slot < 608, slot - 224, slot)
    place = jnp.where(slot < 544, slot + 64, place)
    place = jnp.where(slot < 480, slot - 160, place)
    place = jnp.where(slot < 416, slot + 128, place)
    return jnp.where(slot < NODE, slot, place)


def scatter_far(lat, lon, source, target, send_sem, recv_sem):
    me = lat * N_LON + lon

    def one(step, carry):
        peer = lax.rem(me + step, DEVICES)
        pltpu.make_async_remote_copy(
            src_ref=source.at[peer],
            dst_ref=target.at[me],
            send_sem=send_sem,
            recv_sem=recv_sem,
            device_id=(peer // N_LON, lax.rem(peer, N_LON)),
            device_id_type=MESH,
        ).start()
        return carry

    lax.fori_loop(1, DEVICES, one, 0)


def scatter_half(lat, lon, half, source, target, send_sem, recv_sem):
    me = lat * N_LON + lon

    def one(step, carry):
        peer = 64 * half + lax.rem(me + step, 64)

        @pl.when(peer != me)
        def _():
            pltpu.make_async_remote_copy(
                src_ref=source.at[peer],
                dst_ref=target.at[me],
                send_sem=send_sem,
                recv_sem=recv_sem,
                device_id=(peer // N_LON, lax.rem(peer, N_LON)),
                device_id_type=MESH,
            ).start()

        return carry

    lax.fori_loop(0, 64, one, 0)


def far_waits(source, target, send_sem, recv_sem):
    some = pl.ds(0, DEVICES - 1)
    pltpu.make_async_copy(source.at[some], target.at[some], recv_sem).wait()
    pltpu.make_async_copy(source.at[some], target.at[some], send_sem).wait()


def around(lat, lon, di, dj):
    return (lax.rem(lat + di + N_LAT, N_LAT), lax.rem(lon + dj + N_LON, N_LON))


def group_row(groups):
    return jnp.concatenate([groups[0, a, b : b + 1, :] for a in range(2) for b in range(2)], axis=1)


def columns(rows, target):
    for j in range(EDGE // 128):
        target[128 * j : 128 * j + 128, :] = column(rows[j : j + 1, :])


def silu_parts(pre):
    sig = 0.5 * jnp.tanh(0.5 * pre) + 0.5
    value = pre * sig
    return value, sig + value - value * sig


def normal(values):
    mean = jnp.mean(values, -1, keepdims=True)
    centred = values - mean
    var = jnp.mean(centred * centred, -1, keepdims=True)
    return centred, lax.rsqrt(var + 1e-05)


def pipeline(stages, count):
    for step in range(count + len(stages) - 1):
        for lag, stage in enumerate(stages):
            if 0 <= step - lag < count:
                stage(step - lag)


def send_cells(lat, lon, source, target, inward, cell_send, cell_recv):
    copies = []
    for i, (cell, di, dj, a, b) in enumerate(CELLS):
        if inward:
            kind = 2 * abs(di) + abs(dj) - 1
            src, dst, peer = source.at[i], target.at[kind * 4 + 2 * a + b], (di, dj)
        else:
            src, dst, peer = source.at[(a + 1) * 4 + b + 1], target.at[cell], (-di, -dj)
        copy = pltpu.make_async_remote_copy(
            src_ref=src,
            dst_ref=dst,
            send_sem=cell_send.at[i],
            recv_sem=cell_recv.at[i],
            device_id=around(lat, lon, *peer),
            device_id_type=MESH,
        )
        copy.start()
        copies.append(copy)
    return copies


def layer_kernel(
    count, node_h, groups_h, slots_h, ws_h, wr_h, hidden_bias_h, sender_h, receiver_h, we_h, edge_h,
    wm_h, message_bias_h, edge_scales_h, wself_h, wsum_h, node_bias_h, wu_h, update_bias_h,
    node_scales_h, node_cot_h, cot_h,
    edge_out_h, grad_h, node_out_h, total_h,
    node, groups, slots, ws, wr, hidden_bias, sender, receiver, we, edge,
    wm, message_bias, edge_scales, wself, wsum, node_bias, wu, update_bias,
    node_scales, node_cot, cot,
    border, wide, out, far, table, rproj, scol, rcol, pre,
    hats, slope, rstd, dsummed, node_out, total,
    border_grad, far_grad, far_back, cells_back, by_receiver, by_sender, to_receiver, to_far,
    in_sems, edge_sems, grad_sems, node_sems, far_sems, cell_send, cell_recv, back_send, back_recv,
):
    lat, lon = position()
    me = lat * N_LON + lon
    loads = []
    for i, (src, dst) in enumerate(
        (
            (node_h, node), (groups_h, groups), (slots_h, slots), (ws_h, ws), (wr_h, wr),
            (hidden_bias_h, hidden_bias), (sender_h, sender), (receiver_h, receiver),
            (we_h, we), (edge_h, edge), (wm_h, wm), (message_bias_h, message_bias),
            (edge_scales_h, edge_scales), (wself_h, wself), (wsum_h, wsum),
            (node_bias_h, node_bias), (wu_h, wu), (update_bias_h, update_bias),
            (node_scales_h, node_scales), (node_cot_h, node_cot), (cot_h, cot),
        )
    ):
        loads.append(pltpu.make_async_copy(src, dst, in_sems.at[i]))
    for load in loads[:3]:
        load.start()
    barrier = greet(lat, lon)
    for load in loads[3:]:
        load.start()

    def arrived(first, last):
        for load in loads[first:last]:
            load.wait()

    arrived(0, 3)
    rows = dot(onehot_cols(column(group_row(groups)), 0, NODE), node[...]).astype(BF)
    for a in range(2):
        for b in range(2):
            g = 2 * a + b
            border[(a + 1) * 4 + b + 1] = rows[g * HALO : (g + 1) * HALO]
    for c in range(CAP):
        rows = dot(onehot_cols(column(slots[0, c : c + 1, :]), 0, NODE), node[...])
        for k in range(4):
            wide[pl.ds(4 * c + k, DEVICES, stride=16), :] = rows[:, 128 * k : 128 * k + 128]
    out[...] = wide[...].astype(BF).reshape(DEVICES, 16, 128)
    pl.semaphore_wait(barrier, DEVICES - 1)
    scatter_far(lat, lon, out, far, far_sems.at[0], far_sems.at[1])
    copies = send_cells(lat, lon, border, border, False, cell_send, cell_recv)
    own = pltpu.make_async_copy(out.at[me], far.at[me], far_sems.at[2])
    own.start()
    arrived(3, 10)
    sender[...] = sender_place(sender[...])
    columns(sender, scol)
    columns(receiver, rcol)
    table[0:NODE] = dot(node[...], ws[...]).astype(BF)
    center = jnp.concatenate([border[cell] for cell in (5, 6, 9, 10)], axis=0)
    table[NODE:OUTER] = dot(center, ws[...]).astype(BF)
    rproj[...] = (dot(node[...], wr[...]) + hidden_bias[...]).astype(BF)
    def near(i, carry):
        at = pl.ds(pl.multiple_of(i * TILE, TILE), TILE)
        picked = onehot_cols(rcol[at, :], 0, NODE)
        by_receiver[at, :] = picked
        by_sender[at, :] = onehot_cols(scol[at, :], OUTER, REMOTE)
        pre[at, :] = (
            dot(edge[at, :], we[...])
            + dot(onehot_cols(scol[at, :], 0, OUTER), table[0:OUTER])
            + dot(picked, rproj[...])
        )
        return carry

    lax.fori_loop(0, EDGE // TILE, near, 0)
    for j in range(EDGE // 128):
        at = pl.ds(128 * j, 128)
        to_receiver[:, at] = onehot_rows([receiver[j : j + 1, :]], 0, NODE)
        to_far[:, at] = onehot_rows([sender[j : j + 1, :]], NODE + BORDER, FAR)
    arrived(10, 21)
    total[...] = dot(node[...], wself[...]) + node_bias[...]
    for copy in copies:
        copy.wait()
    cells = [border[0:5], border[7:9], border[11:16]]
    cells = jnp.concatenate([c.reshape(-1, D) for c in cells], axis=0)
    table[OUTER : NODE + BORDER] = dot(cells, ws[...]).astype(BF)
    own.wait()
    far_waits(out, far, far_sems.at[0], far_sems.at[1])
    wide[...] = far[...].reshape(FAR * 4, 128).astype(F32)
    for h in range(2):
        rows = jnp.concatenate(
            [wide[pl.ds(1024 * h + k, 256, stride=4), :].astype(BF) for k in range(4)], axis=1
        )
        table[pl.ds(NODE + BORDER + 256 * h, 256)] = dot(rows, ws[...]).astype(BF)
    live_edges = count[0]

    senders = [sender[j : j + 1, :] for j in range(EDGE // 128)]
    tiles = [pl.ds(i * TILE, TILE) for i in range(EDGE // TILE)]
    halves = [{} for _ in tiles]
    summed = jnp.zeros((NODE, D), F32)

    def inputs(i):
        at = tiles[i]
        halves[i]["pre"] = pre[at, :] + dot(by_sender[at, :], table[OUTER : OUTER + REMOTE])

    def activate(i):
        value, grad = silu_parts(halves[i]["pre"])
        slope[tiles[i], :] = grad.astype(BF)
        halves[i]["value"] = value.astype(BF)

    def project(i):
        halves[i]["message"] = dot(halves[i]["value"], wm[...]) + message_bias[...]

    def normalise(i):
        at = tiles[i]
        centred, scale = normal(halves[i]["message"])
        place = lax.broadcasted_iota(jnp.int32, (TILE, 1), 0) + i * TILE
        scale = jnp.where(place < live_edges, scale, 0.0)
        rstd[at, :] = scale
        hat = centred * scale
        hats[at, :] = hat.astype(BF)
        said = hat * edge_scales[...]
        halves[i]["said"] = said.astype(BF)
        edge[at, :] = (edge[at, :].astype(F32) + said).astype(BF)
        pltpu.make_async_copy(edge.at[at, :], edge_out_h.at[at, :], edge_sems.at[i]).start()

    def gather_sum(i):
        nonlocal summed
        summed = summed + dot(to_receiver[:, tiles[i]], halves[i]["said"])

    pipeline((inputs, activate, project, normalise, gather_sum), len(tiles))
    summed = summed.astype(BF)
    value, grad = silu_parts(total[...] + dot(summed, wsum[...]))
    centred, scale = normal(dot(value.astype(BF), wu[...]) + update_bias[...])
    hat = centred * scale
    node_out[...] = (node[...].astype(F32) + hat * node_scales[...]).astype(BF)
    node_copy = pltpu.make_async_copy(node_out, node_out_h, node_sems.at[0])
    node_copy.start()
    upper = node_cot[...].astype(F32)
    g = upper * node_scales[...]
    back = scale * (
        g - jnp.mean(g, -1, keepdims=True) - hat * jnp.mean(g * hat, -1, keepdims=True)
    )
    inner = (dot_t(back.astype(BF), wu[...]) * grad).astype(BF)
    dsummed[...] = dot_t(inner, wsum[...]).astype(BF)
    total[...] = upper + dot_t(inner, wself[...])

    far_rows = jnp.zeros((FAR, D), F32)

    def spread(i):
        at = tiles[i]
        halves[i]["grad"] = dot(by_receiver[at, :], dsummed[...])

    def denormalise(i):
        at = tiles[i]
        g = (cot[at, :].astype(F32) + halves[i]["grad"]) * edge_scales[...]
        hat = hats[at, :].astype(F32)
        back = rstd[at, :] * (
            g - jnp.mean(g, -1, keepdims=True) - hat * jnp.mean(g * hat, -1, keepdims=True)
        )
        halves[i]["back"] = back.astype(BF)

    def unproject(i):
        halves[i]["hidden"] = dot_t(halves[i]["back"], wm[...])

    def deactivate(i):
        at = tiles[i]
        hats[at, :] = (halves[i]["hidden"] * slope[at, :].astype(F32)).astype(BF)

    def gather_far(i):
        nonlocal far_rows
        far_rows = far_rows + dot(to_far[:, tiles[i]], hats[tiles[i], :])

    pipeline((spread, denormalise, unproject, deactivate, gather_far), len(tiles))
    far_rows = far_rows.astype(BF)

    for h in range(2):
        rows = dot_t(far_rows[256 * h : 256 * h + 256], ws[...])
        for k in range(4):
            wide[pl.ds(1024 * h + k, 256, stride=4), :] = rows[:, 128 * k : 128 * k + 128]
        part = wide[1024 * h : 1024 * h + 1024, :].astype(BF)
        far_grad[64 * h : 64 * h + 64] = part.reshape(64, 16, 128)
        scatter_half(lat, lon, h, far_grad, far_back, far_sems.at[3], far_sems.at[4])
    own = pltpu.make_async_copy(far_grad.at[me], far_back.at[me], far_sems.at[5])
    own.start()
    rows = dot(onehot_rows(senders, OUTER, 12 * HALO), hats[...]).astype(BF)
    border_grad[...] = dot_t(rows, ws[...]).astype(BF).reshape(12, HALO, D)
    copies = send_cells(lat, lon, border_grad, cells_back, True, back_send, back_recv)
    received = dot(to_receiver[...], hats[...]).astype(BF)
    picked = onehot_rows([group_row(groups)], 0, NODE)
    rows = dot(onehot_rows(senders, 0, OUTER), hats[...])
    rows = rows[0:NODE] + dot(picked, rows[NODE:OUTER].astype(BF))
    total[...] += dot_t(rows.astype(BF), ws[...]) + dot_t(received, wr[...])

    def grads(i, carry):
        at = pl.ds(pl.multiple_of(i * TILE, TILE), TILE)
        pre[at, :] = cot[at, :].astype(F32) + dot_t(hats[at, :], we[...])
        pltpu.make_async_copy(pre.at[at, :], grad_h.at[at, :], grad_sems.at[i]).start()
        return carry

    lax.fori_loop(0, EDGE // TILE, grads, 0)
    for copy in copies:
        copy.wait()
    summed = dot(picked, cells_back[0:4].reshape(128, D))
    for kind in (1, 2):
        summed = summed + dot(picked, cells_back[4 * kind : 4 * kind + 4].reshape(128, D))
    total[...] += summed
    own.wait()
    far_waits(far_grad, far_back, far_sems.at[3], far_sems.at[4])
    wide[...] = far_back[...].reshape(FAR * 4, 128).astype(F32)
    returned = jnp.concatenate(
        [
            jnp.concatenate(
                [wide[pl.ds(4 * c + k, DEVICES, stride=16), :].astype(BF) for k in range(4)], axis=1
            )
            for c in range(CAP)
        ],
        axis=0,
    )
    lists = onehot_rows([slots[0, c : c + 1, :] for c in range(CAP)], 0, NODE)
    total[...] += dot(lists, returned)
    total_copy = pltpu.make_async_copy(total, total_h, node_sems.at[1])
    total_copy.start()
    for i in range(EDGE // TILE):
        at = pl.ds(i * TILE, TILE)
        pltpu.make_async_copy(edge.at[at, :], edge_out_h.at[at, :], edge_sems.at[i]).wait()
        pltpu.make_async_copy(pre.at[at, :], grad_h.at[at, :], grad_sems.at[i]).wait()
    node_copy.wait()
    total_copy.wait()


def finish_kernel(edge_i, grad_i, node_i, total_i, edge_o, grad_o, node_o, total_o, sems):
    copies = []
    for i in range(8):
        at = pl.ds(i * (EDGE // 8), EDGE // 8)
        copies.append((grad_i.at[at, :], grad_o.at[at, :]))
    for i in range(4):
        at = pl.ds(i * (EDGE // 4), EDGE // 4)
        copies.append((edge_i.at[at, :], edge_o.at[at, :]))
    copies += [(total_i, total_o), (node_i, node_o)]
    copies = [pltpu.make_async_copy(*pair, sems.at[i]) for i, pair in enumerate(copies)]
    for copy in copies:
        copy.start()
    for copy in copies:
        copy.wait()


def vmem(count):
    return [pl.BlockSpec(memory_space=pltpu.VMEM)] * count


def per_device(
    node_latent, edge_latent, sender_slot, receiver, border_list, send_list, edge_count,
    edge_weight, sender_weight, receiver_weight, hidden_bias, message_weight, message_bias,
    edge_scales, self_weight, summed_weight, node_bias, update_weight, update_bias, node_scales,
    node_cotangent, edge_cotangent,
):
    slots = send_list.transpose(0, 2, 1)
    sender = sender_slot.reshape(EDGE // 128, 128)
    receiver = receiver.reshape(EDGE // 128, 128)
    sems = pltpu.SemaphoreType.DMA
    tiles = sems((EDGE // TILE,))
    cells = pltpu.VMEM((16, HALO, D), BF)
    chunk = pltpu.VMEM((DEVICES, 16, 128), BF)
    wide = pltpu.VMEM((FAR * 4, 128), F32)
    weight = pltpu.VMEM((D, D), BF)
    half = pltpu.VMEM((EDGE, D), BF)
    full = pltpu.VMEM((EDGE, D), F32)
    nodes = pltpu.VMEM((NODE, D), BF)
    column_of = pltpu.VMEM((EDGE, 128), jnp.int32)
    any_space = pl.BlockSpec(memory_space=pl.ANY)
    hbm = pl.BlockSpec(memory_space=pltpu.HBM)
    line = pltpu.VMEM((1, D), F32)
    outer = pltpu.VMEM((12, HALO, D), BF)
    slot_rows = pltpu.VMEM((EDGE // 128, 128), jnp.int32)
    keep = lambda v: pltpu.with_memory_space_constraint(v, pltpu.HBM)
    vector = lambda v: v.reshape(1, D)
    results = (
        jax.ShapeDtypeStruct((EDGE, D), BF),
        jax.ShapeDtypeStruct((EDGE, D), F32),
        jax.ShapeDtypeStruct((NODE, D), BF),
        jax.ShapeDtypeStruct((NODE, D), F32),
    )
    done = pl.pallas_call(
        layer_kernel,
        out_shape=results,
        in_specs=[pl.BlockSpec(memory_space=pltpu.SMEM)] + [hbm] * 21,
        out_specs=(any_space,) * 4,
        scratch_shapes=[
            nodes, pltpu.VMEM((1, 2, 2, HALO), jnp.int32), pltpu.VMEM((1, CAP, DEVICES), jnp.int32),
            weight, weight, line, slot_rows, slot_rows, weight, half,
            weight, line, line, weight, weight, line, weight, line, line, nodes, half,
        ]
        + [
            cells, wide, chunk, chunk, pltpu.VMEM((NODE + BORDER + FAR, D), BF), nodes,
            column_of, column_of, full,
            half, half, pltpu.VMEM((EDGE, 1), F32), nodes, nodes,
            pltpu.VMEM((NODE, D), F32),
            outer, chunk, chunk, outer,
            pltpu.VMEM((EDGE, NODE), BF), pltpu.VMEM((EDGE, REMOTE), BF),
            pltpu.VMEM((NODE, EDGE), BF), pltpu.VMEM((FAR, EDGE), BF),
            sems((21,)), tiles, tiles, sems((2,)), sems((6,)),
            sems((12,)), sems((12,)), sems((12,)), sems((12,)),
        ],
        compiler_params=pltpu.CompilerParams(
            collective_id=0, has_side_effects=True, vmem_limit_bytes=LIMIT
        ),
        name="layer",
    )(
        edge_count,
        *map(keep, (
        node_latent, border_list, slots, sender_weight, receiver_weight,
        vector(hidden_bias), sender, receiver, edge_weight, edge_latent,
        message_weight, vector(message_bias), vector(edge_scales), self_weight, summed_weight,
        vector(node_bias), update_weight, vector(update_bias), vector(node_scales),
        node_cotangent, edge_cotangent,
        )),
    )
    edge_result, edge_grad, node_result, node_grad = pl.pallas_call(
        finish_kernel,
        out_shape=results,
        in_specs=[any_space] * 4,
        out_specs=(any_space,) * 4,
        scratch_shapes=[sems((14,))],
        compiler_params=pltpu.CompilerParams(vmem_limit_bytes=1024 * 1024),
        name="finish",
    )(*done)
    return node_result, edge_result, node_grad, edge_grad


def solution(mesh):
    both = ("lat", "lon")
    placed = (
        P(both, None), P(both, None), P(both), P(both), P(both, None, None, None),
        P(both, None, None), P(both),
        P(), P(), P(), P(), P(), P(), P(), P(), P(), P(), P(), P(), P(),
        P(both, None), P(both, None),
    )
    return jax.shard_map(
        per_device,
        mesh=mesh,
        in_specs=placed,
        out_specs=(P(both, None),) * 4,
        check_vma=False,
    )
```

```python
import functools

import jax
import jax.numpy as jnp
from jax import lax
from jax.experimental import pallas as pl
from jax.experimental.pallas import tpu as pltpu
from jax.sharding import PartitionSpec as P

BF = jnp.bfloat16
F32 = jnp.float32
MESH = pl.DeviceIdType.MESH
N_LAT, N_LON = 8, 16
DEVICES = 128
D = 512
NODE = 256
EDGE = 2048
HALO = 32
CAP = 4
FAR = DEVICES * CAP
BORDER = 16 * HALO
TILE = 1024
LIMIT = 46 * 1024 * 1024
OUTER = NODE + 4 * HALO
REMOTE = 12 * HALO + FAR

def _owner(row):
    return (-1, 1) if row == 0 else (1, 0) if row == 3 else (0, row - 1)


CELLS = []
for _r in range(4):
    for _s in range(4):
        _di, _a = _owner(_r)
        _dj, _b = _owner(_s)
        if _di or _dj:
            CELLS.append((_r * 4 + _s, _di, _dj, _a, _b))


def dot(a, b):
    return jnp.dot(a, b, preferred_element_type=F32)


def dot_t(a, b):
    return lax.dot_general(a, b, (((1,), (1,)), ((), ())), preferred_element_type=F32)


def column(row):
    return jnp.transpose(jnp.broadcast_to(row, (128, 128)))


def onehot_cols(col, base, width):
    lane = lax.broadcasted_iota(jnp.int32, col.shape, 1)
    parts = [
        jnp.where(col == lane + (base + k), 1.0, 0.0).astype(BF) for k in range(0, width, 128)
    ]
    return jnp.concatenate(parts, axis=1)


def onehot_rows(rows, base, height):
    parts = []
    for row in rows:
        place = lax.broadcasted_iota(jnp.int32, (height, 128), 0) + base
        parts.append(jnp.where(place == row, 1.0, 0.0).astype(BF))
    return jnp.concatenate(parts, axis=1) if len(parts) > 1 else parts[0]


def position():
    return lax.axis_index("lat"), lax.axis_index("lon")


def greet(lat, lon):
    barrier = pltpu.get_barrier_semaphore()
    lats = [lax.rem(lat + i, N_LAT) for i in range(N_LAT)]
    lons = [lax.rem(lon + j, N_LON) for j in range(N_LON)]
    for j in range(N_LON):
        for i in range(N_LAT):
            if i or j:
                pl.semaphore_signal(
                    barrier, inc=1, device_id=(lats[i], lons[j]), device_id_type=MESH
                )
    return barrier


def sender_place(slot):
    place = jnp.where(slot < 608, slot - 224, slot)
    place = jnp.where(slot < 544, slot + 64, place)
    place = jnp.where(slot < 480, slot - 160, place)
    place = jnp.where(slot < 416, slot + 128, place)
    return jnp.where(slot < NODE, slot, place)


def scatter_far(lat, lon, source, target, send_sem, recv_sem):
    me = lat * N_LON + lon

    def one(step, carry):
        apart = DEVICES // 2 + (step // 2) * (1 - 2 * lax.rem(step, 2))
        peer = lax.rem(me + apart, DEVICES)
        pltpu.make_async_remote_copy(
            src_ref=source.at[peer],
            dst_ref=target.at[me],
            send_sem=send_sem,
            recv_sem=recv_sem,
            device_id=(peer // N_LON, lax.rem(peer, N_LON)),
            device_id_type=MESH,
        ).start()
        return carry

    lax.fori_loop(1, DEVICES, one, 0)


def scatter_half(lat, lon, half, source, target, send_sem, recv_sem):
    me = lat * N_LON + lon

    def one(step, carry):
        peer = 64 * half + lax.rem(me + step, 64)

        @pl.when(peer != me)
        def _():
            pltpu.make_async_remote_copy(
                src_ref=source.at[peer],
                dst_ref=target.at[me],
                send_sem=send_sem,
                recv_sem=recv_sem,
                device_id=(peer // N_LON, lax.rem(peer, N_LON)),
                device_id_type=MESH,
            ).start()

        return carry

    lax.fori_loop(0, 64, one, 0)


def far_waits(source, target, send_sem, recv_sem):
    some = pl.ds(0, DEVICES - 1)
    pltpu.make_async_copy(source.at[some], target.at[some], recv_sem).wait()
    pltpu.make_async_copy(source.at[some], target.at[some], send_sem).wait()


def around(lat, lon, di, dj):
    return (lax.rem(lat + di + N_LAT, N_LAT), lax.rem(lon + dj + N_LON, N_LON))


def group_row(groups):
    return jnp.concatenate([groups[0, a, b : b + 1, :] for a in range(2) for b in range(2)], axis=1)


def columns(rows, target):
    for j in range(EDGE // 128):
        target[128 * j : 128 * j + 128, :] = column(rows[j : j + 1, :])


def silu_parts(pre):
    sig = 0.5 * jnp.tanh(0.5 * pre) + 0.5
    value = pre * sig
    return value, sig + value - value * sig


def normal(values):
    mean = jnp.mean(values, -1, keepdims=True)
    centred = values - mean
    var = jnp.mean(centred * centred, -1, keepdims=True)
    return centred, lax.rsqrt(var + 1e-05)


def pipeline(stages, count):
    for step in range(count + len(stages) - 1):
        for lag, stage in enumerate(stages):
            if 0 <= step - lag < count:
                stage(step - lag)


def send_cells(lat, lon, source, target, inward, cell_send, cell_recv):
    copies = []
    for i, (cell, di, dj, a, b) in enumerate(CELLS):
        if inward:
            kind = 2 * abs(di) + abs(dj) - 1
            src, dst, peer = source.at[i], target.at[kind * 4 + 2 * a + b], (di, dj)
        else:
            src, dst, peer = source.at[(a + 1) * 4 + b + 1], target.at[cell], (-di, -dj)
        copy = pltpu.make_async_remote_copy(
            src_ref=src,
            dst_ref=dst,
            send_sem=cell_send.at[i],
            recv_sem=cell_recv.at[i],
            device_id=around(lat, lon, *peer),
            device_id_type=MESH,
        )
        copy.start()
        copies.append(copy)
    return copies


def layer_kernel(
    count, node_h, groups_h, slots_h, ws_h, wr_h, hidden_bias_h, sender_h, receiver_h, we_h, edge_h,
    wm_h, message_bias_h, edge_scales_h, wself_h, wsum_h, node_bias_h, wu_h, update_bias_h,
    node_scales_h, node_cot_h, cot_h,
    edge_out_h, grad_h, node_out_h, total_h,
    node, groups, slots, ws, wr, hidden_bias, sender, receiver, we, edge,
    wm, message_bias, edge_scales, wself, wsum, node_bias, wu, update_bias,
    node_scales, node_cot, cot,
    border, wide, out, far, table, rproj, scol, rcol, pre,
    hats, slope, rstd, dsummed, node_out, total,
    border_grad, far_grad, far_back, cells_back, by_receiver, by_sender, to_receiver, to_far,
    in_sems, edge_sems, grad_sems, node_sems, far_sems, cell_send, cell_recv, back_send, back_recv,
):
    lat, lon = position()
    me = lat * N_LON + lon
    loads = []
    for i, (src, dst) in enumerate(
        (
            (node_h, node), (groups_h, groups), (slots_h, slots), (ws_h, ws), (wr_h, wr),
            (hidden_bias_h, hidden_bias), (sender_h, sender), (receiver_h, receiver),
            (we_h, we), (edge_h, edge), (wm_h, wm), (message_bias_h, message_bias),
            (edge_scales_h, edge_scales), (wself_h, wself), (wsum_h, wsum),
            (node_bias_h, node_bias), (wu_h, wu), (update_bias_h, update_bias),
            (node_scales_h, node_scales), (node_cot_h, node_cot), (cot_h, cot),
        )
    ):
        loads.append(pltpu.make_async_copy(src, dst, in_sems.at[i]))
    for load in loads[:3]:
        load.start()
    barrier = greet(lat, lon)
    for load in loads[3:]:
        load.start()

    def arrived(first, last):
        for load in loads[first:last]:
            load.wait()

    arrived(0, 3)
    rows = dot(onehot_cols(column(group_row(groups)), 0, NODE), node[...]).astype(BF)
    for a in range(2):
        for b in range(2):
            g = 2 * a + b
            border[(a + 1) * 4 + b + 1] = rows[g * HALO : (g + 1) * HALO]
    for c in range(CAP):
        rows = dot(onehot_cols(column(slots[0, c : c + 1, :]), 0, NODE), node[...])
        for k in range(4):
            wide[pl.ds(4 * c + k, DEVICES, stride=16), :] = rows[:, 128 * k : 128 * k + 128]
    out[...] = wide[...].astype(BF).reshape(DEVICES, 16, 128)
    pl.semaphore_wait(barrier, DEVICES - 1)
    scatter_far(lat, lon, out, far, far_sems.at[0], far_sems.at[1])
    copies = send_cells(lat, lon, border, border, False, cell_send, cell_recv)
    own = pltpu.make_async_copy(out.at[me], far.at[me], far_sems.at[2])
    own.start()
    arrived(3, 10)
    sender[...] = sender_place(sender[...])
    columns(sender, scol)
    columns(receiver, rcol)
    table[0:NODE] = dot(node[...], ws[...]).astype(BF)
    center = jnp.concatenate([border[cell] for cell in (5, 6, 9, 10)], axis=0)
    table[NODE:OUTER] = dot(center, ws[...]).astype(BF)
    rproj[...] = (dot(node[...], wr[...]) + hidden_bias[...]).astype(BF)
    def near(i, carry):
        at = pl.ds(pl.multiple_of(i * TILE, TILE), TILE)
        picked = onehot_cols(rcol[at, :], 0, NODE)
        by_receiver[at, :] = picked
        by_sender[at, :] = onehot_cols(scol[at, :], OUTER, REMOTE)
        pre[at, :] = (
            dot(edge[at, :], we[...])
            + dot(onehot_cols(scol[at, :], 0, OUTER), table[0:OUTER])
            + dot(picked, rproj[...])
        )
        return carry

    lax.fori_loop(0, EDGE // TILE, near, 0)
    for j in range(EDGE // 128):
        at = pl.ds(128 * j, 128)
        to_receiver[:, at] = onehot_rows([receiver[j : j + 1, :]], 0, NODE)
        to_far[:, at] = onehot_rows([sender[j : j + 1, :]], NODE + BORDER, FAR)
    arrived(10, 21)
    total[...] = dot(node[...], wself[...]) + node_bias[...]
    for copy in copies:
        copy.wait()
    cells = [border[0:5], border[7:9], border[11:16]]
    cells = jnp.concatenate([c.reshape(-1, D) for c in cells], axis=0)
    table[OUTER : NODE + BORDER] = dot(cells, ws[...]).astype(BF)
    own.wait()
    far_waits(out, far, far_sems.at[0], far_sems.at[1])
    wide[...] = far[...].reshape(FAR * 4, 128).astype(F32)
    for h in range(2):
        rows = jnp.concatenate(
            [wide[pl.ds(1024 * h + k, 256, stride=4), :].astype(BF) for k in range(4)], axis=1
        )
        table[pl.ds(NODE + BORDER + 256 * h, 256)] = dot(rows, ws[...]).astype(BF)
    live_edges = count[0]

    senders = [sender[j : j + 1, :] for j in range(EDGE // 128)]
    tiles = [pl.ds(i * TILE, TILE) for i in range(EDGE // TILE)]
    halves = [{} for _ in tiles]
    summed = jnp.zeros((NODE, D), F32)

    def inputs(i):
        at = tiles[i]
        halves[i]["pre"] = pre[at, :] + dot(by_sender[at, :], table[OUTER : OUTER + REMOTE])

    def activate(i):
        value, grad = silu_parts(halves[i]["pre"])
        slope[tiles[i], :] = grad.astype(BF)
        halves[i]["value"] = value.astype(BF)

    def project(i):
        halves[i]["message"] = dot(halves[i]["value"], wm[...]) + message_bias[...]

    def normalise(i):
        at = tiles[i]
        centred, scale = normal(halves[i]["message"])
        place = lax.broadcasted_iota(jnp.int32, (TILE, 1), 0) + i * TILE
        scale = jnp.where(place < live_edges, scale, 0.0)
        rstd[at, :] = scale
        hat = centred * scale
        hats[at, :] = hat.astype(BF)
        said = hat * edge_scales[...]
        halves[i]["said"] = said.astype(BF)
        edge[at, :] = (edge[at, :].astype(F32) + said).astype(BF)
        pltpu.make_async_copy(edge.at[at, :], edge_out_h.at[at, :], edge_sems.at[i]).start()

    def gather_sum(i):
        nonlocal summed
        summed = summed + dot(to_receiver[:, tiles[i]], halves[i]["said"])

    pipeline((inputs, activate, project, normalise, gather_sum), len(tiles))
    summed = summed.astype(BF)
    value, grad = silu_parts(total[...] + dot(summed, wsum[...]))
    centred, scale = normal(dot(value.astype(BF), wu[...]) + update_bias[...])
    hat = centred * scale
    node_out[...] = (node[...].astype(F32) + hat * node_scales[...]).astype(BF)
    node_copy = pltpu.make_async_copy(node_out, node_out_h, node_sems.at[0])
    node_copy.start()
    upper = node_cot[...].astype(F32)
    g = upper * node_scales[...]
    back = scale * (
        g - jnp.mean(g, -1, keepdims=True) - hat * jnp.mean(g * hat, -1, keepdims=True)
    )
    inner = (dot_t(back.astype(BF), wu[...]) * grad).astype(BF)
    dsummed[...] = dot_t(inner, wsum[...]).astype(BF)
    total[...] = upper + dot_t(inner, wself[...])

    far_rows = jnp.zeros((FAR, D), F32)

    def spread(i):
        at = tiles[i]
        halves[i]["grad"] = dot(by_receiver[at, :], dsummed[...])

    def denormalise(i):
        at = tiles[i]
        g = (cot[at, :].astype(F32) + halves[i]["grad"]) * edge_scales[...]
        hat = hats[at, :].astype(F32)
        back = rstd[at, :] * (
            g - jnp.mean(g, -1, keepdims=True) - hat * jnp.mean(g * hat, -1, keepdims=True)
        )
        halves[i]["back"] = back.astype(BF)

    def unproject(i):
        halves[i]["hidden"] = dot_t(halves[i]["back"], wm[...])

    def deactivate(i):
        at = tiles[i]
        hats[at, :] = (halves[i]["hidden"] * slope[at, :].astype(F32)).astype(BF)

    def gather_far(i):
        nonlocal far_rows
        far_rows = far_rows + dot(to_far[:, tiles[i]], hats[tiles[i], :])

    pipeline((spread, denormalise, unproject, deactivate, gather_far), len(tiles))
    far_rows = far_rows.astype(BF)

    for h in range(2):
        rows = dot_t(far_rows[256 * h : 256 * h + 256], ws[...])
        for k in range(4):
            wide[pl.ds(1024 * h + k, 256, stride=4), :] = rows[:, 128 * k : 128 * k + 128]
        part = wide[1024 * h : 1024 * h + 1024, :].astype(BF)
        far_grad[64 * h : 64 * h + 64] = part.reshape(64, 16, 128)
        scatter_half(lat, lon, h, far_grad, far_back, far_sems.at[3], far_sems.at[4])
    own = pltpu.make_async_copy(far_grad.at[me], far_back.at[me], far_sems.at[5])
    own.start()
    rows = dot(onehot_rows(senders, OUTER, 12 * HALO), hats[...]).astype(BF)
    border_grad[...] = dot_t(rows, ws[...]).astype(BF).reshape(12, HALO, D)
    copies = send_cells(lat, lon, border_grad, cells_back, True, back_send, back_recv)
    received = dot(to_receiver[...], hats[...]).astype(BF)
    picked = onehot_rows([group_row(groups)], 0, NODE)
    rows = dot(onehot_rows(senders, 0, OUTER), hats[...])
    rows = rows[0:NODE] + dot(picked, rows[NODE:OUTER].astype(BF))
    total[...] += dot_t(rows.astype(BF), ws[...]) + dot_t(received, wr[...])

    def grads(i, carry):
        at = pl.ds(pl.multiple_of(i * TILE, TILE), TILE)
        pre[at, :] = cot[at, :].astype(F32) + dot_t(hats[at, :], we[...])
        pltpu.make_async_copy(pre.at[at, :], grad_h.at[at, :], grad_sems.at[i]).start()
        return carry

    lax.fori_loop(0, EDGE // TILE, grads, 0)
    for copy in copies:
        copy.wait()
    summed = dot(picked, cells_back[0:4].reshape(128, D))
    for kind in (1, 2):
        summed = summed + dot(picked, cells_back[4 * kind : 4 * kind + 4].reshape(128, D))
    total[...] += summed
    own.wait()
    far_waits(far_grad, far_back, far_sems.at[3], far_sems.at[4])
    wide[...] = far_back[...].reshape(FAR * 4, 128).astype(F32)
    returned = jnp.concatenate(
        [
            jnp.concatenate(
                [wide[pl.ds(4 * c + k, DEVICES, stride=16), :].astype(BF) for k in range(4)], axis=1
            )
            for c in range(CAP)
        ],
        axis=0,
    )
    lists = onehot_rows([slots[0, c : c + 1, :] for c in range(CAP)], 0, NODE)
    total[...] += dot(lists, returned)
    total_copy = pltpu.make_async_copy(total, total_h, node_sems.at[1])
    total_copy.start()
    for i in range(EDGE // TILE):
        at = pl.ds(i * TILE, TILE)
        pltpu.make_async_copy(edge.at[at, :], edge_out_h.at[at, :], edge_sems.at[i]).wait()
        pltpu.make_async_copy(pre.at[at, :], grad_h.at[at, :], grad_sems.at[i]).wait()
    node_copy.wait()
    total_copy.wait()


def finish_kernel(edge_i, grad_i, node_i, total_i, edge_o, grad_o, node_o, total_o, sems):
    copies = []
    for i in range(8):
        at = pl.ds(i * (EDGE // 8), EDGE // 8)
        copies.append((grad_i.at[at, :], grad_o.at[at, :]))
    for i in range(4):
        at = pl.ds(i * (EDGE // 4), EDGE // 4)
        copies.append((edge_i.at[at, :], edge_o.at[at, :]))
    copies += [(total_i, total_o), (node_i, node_o)]
    copies = [pltpu.make_async_copy(*pair, sems.at[i]) for i, pair in enumerate(copies)]
    for copy in copies:
        copy.start()
    for copy in copies:
        copy.wait()


def vmem(count):
    return [pl.BlockSpec(memory_space=pltpu.VMEM)] * count


def per_device(
    node_latent, edge_latent, sender_slot, receiver, border_list, send_list, edge_count,
    edge_weight, sender_weight, receiver_weight, hidden_bias, message_weight, message_bias,
    edge_scales, self_weight, summed_weight, node_bias, update_weight, update_bias, node_scales,
    node_cotangent, edge_cotangent,
):
    slots = send_list.transpose(0, 2, 1)
    sender = sender_slot.reshape(EDGE // 128, 128)
    receiver = receiver.reshape(EDGE // 128, 128)
    sems = pltpu.SemaphoreType.DMA
    tiles = sems((EDGE // TILE,))
    cells = pltpu.VMEM((16, HALO, D), BF)
    chunk = pltpu.VMEM((DEVICES, 16, 128), BF)
    wide = pltpu.VMEM((FAR * 4, 128), F32)
    weight = pltpu.VMEM((D, D), BF)
    half = pltpu.VMEM((EDGE, D), BF)
    full = pltpu.VMEM((EDGE, D), F32)
    nodes = pltpu.VMEM((NODE, D), BF)
    column_of = pltpu.VMEM((EDGE, 128), jnp.int32)
    any_space = pl.BlockSpec(memory_space=pl.ANY)
    hbm = pl.BlockSpec(memory_space=pltpu.HBM)
    line = pltpu.VMEM((1, D), F32)
    outer = pltpu.VMEM((12, HALO, D), BF)
    slot_rows = pltpu.VMEM((EDGE // 128, 128), jnp.int32)
    keep = lambda v: pltpu.with_memory_space_constraint(v, pltpu.HBM)
    vector = lambda v: v.reshape(1, D)
    results = (
        jax.ShapeDtypeStruct((EDGE, D), BF),
        jax.ShapeDtypeStruct((EDGE, D), F32),
        jax.ShapeDtypeStruct((NODE, D), BF),
        jax.ShapeDtypeStruct((NODE, D), F32),
    )
    done = pl.pallas_call(
        layer_kernel,
        out_shape=results,
        in_specs=[pl.BlockSpec(memory_space=pltpu.SMEM)] + [hbm] * 21,
        out_specs=(any_space,) * 4,
        scratch_shapes=[
            nodes, pltpu.VMEM((1, 2, 2, HALO), jnp.int32), pltpu.VMEM((1, CAP, DEVICES), jnp.int32),
            weight, weight, line, slot_rows, slot_rows, weight, half,
            weight, line, line, weight, weight, line, weight, line, line, nodes, half,
        ]
        + [
            cells, wide, chunk, chunk, pltpu.VMEM((NODE + BORDER + FAR, D), BF), nodes,
            column_of, column_of, full,
            half, half, pltpu.VMEM((EDGE, 1), F32), nodes, nodes,
            pltpu.VMEM((NODE, D), F32),
            outer, chunk, chunk, outer,
            pltpu.VMEM((EDGE, NODE), BF), pltpu.VMEM((EDGE, REMOTE), BF),
            pltpu.VMEM((NODE, EDGE), BF), pltpu.VMEM((FAR, EDGE), BF),
            sems((21,)), tiles, tiles, sems((2,)), sems((6,)),
            sems((12,)), sems((12,)), sems((12,)), sems((12,)),
        ],
        compiler_params=pltpu.CompilerParams(
            collective_id=0, has_side_effects=True, vmem_limit_bytes=LIMIT
        ),
        name="layer",
    )(
        edge_count,
        *map(keep, (
        node_latent, border_list, slots, sender_weight, receiver_weight,
        vector(hidden_bias), sender, receiver, edge_weight, edge_latent,
        message_weight, vector(message_bias), vector(edge_scales), self_weight, summed_weight,
        vector(node_bias), update_weight, vector(update_bias), vector(node_scales),
        node_cotangent, edge_cotangent,
        )),
    )
    edge_result, edge_grad, node_result, node_grad = pl.pallas_call(
        finish_kernel,
        out_shape=results,
        in_specs=[any_space] * 4,
        out_specs=(any_space,) * 4,
        scratch_shapes=[sems((14,))],
        compiler_params=pltpu.CompilerParams(vmem_limit_bytes=1024 * 1024),
        name="finish",
    )(*done)
    return node_result, edge_result, node_grad, edge_grad


def solution(mesh):
    both = ("lat", "lon")
    placed = (
        P(both, None), P(both, None), P(both), P(both), P(both, None, None, None),
        P(both, None, None), P(both),
        P(), P(), P(), P(), P(), P(), P(), P(), P(), P(), P(), P(), P(),
        P(both, None), P(both, None),
    )
    return jax.shard_map(
        per_device,
        mesh=mesh,
        in_specs=placed,
        out_specs=(P(both, None),) * 4,
        check_vma=False,
    )
```
